32 devices in a mesh: narrow: 2 (over core), wide: 16 (over z, y, x).
Axes of the slice: x: 2, y: 2, z: 4, core: 2. Of those that a mesh axis runs over, the one named last changes fastest.
Arguments:
- rows: bfloat16 [98304, 1024], P(('narrow', 'wide')), may hold values from -20 to 20
- list_ids: int32 [98304], P(('narrow', 'wide')), may hold values from 0 to 16383, as said below
- codes: int32 [98304, 64], P(('narrow', 'wide')), may hold values from 0 to 255
- row_counts: int32 [32], P(('narrow', 'wide')), may hold values from 1536 to 3072, as said below
- centroids: bfloat16 [16384, 1024], P('wide'), may hold values from -4 to 4
- old_codebook: float32 [64, 4096], replicated, may hold values from -4 to 4
Outputs:
- codebook: float32 [64, 4096], replicated
- search_table: bfloat16 [64, 4096], P('wide')
- row_error: float32 [98304], P(('narrow', 'wide'))
The draws below stay inside these ranges and needn't reach their ends.
Inputs may be any that keep to these rules, and one draw needn't show every extreme that they name: `list_ids`: among the live passages of one device, at most 384 have lists owned by any one index w of wide (lists w * 1024 to (w + 1) * 1024 - 1), and one index of wide receives exactly 384 live passages from every device. Entries past a device's count are arbitrary. `row_counts`: one device holds exactly 3072 live passages.
All inputs are finite; a program needn't handle non-finite values.
Results may differ from the reference program's by a relative error of at most 0.00165.
Values may be sent and summed in bfloat16 or wider, within the bound.
A program may use at most 192 MiB of HBM per device.

```python
import jax
import jax.numpy as jnp
from jax import lax

D = 1024
M = 64
K = 256
DSUB = 16
LISTS_DEV = 1024
LISTS = 16384
ROWS_DEV = 3072
ROWS = 98304
CAP = 384
ANCHOR = 96
N_WIDE = 16
DEVICES = 32


def route_plan(key):
    key_count = jax.random.fold_in(key, 1)
    key_full = jax.random.fold_in(key, 2)
    key_hot = jax.random.fold_in(key, 3)
    key_offset = jax.random.fold_in(key, 4)
    key_order = jax.random.fold_in(key, 5)
    counts = jax.random.randint(key_count, (DEVICES,), ROWS_DEV // 2, ROWS_DEV + 1)
    full_device = jax.random.randint(key_full, (), 0, DEVICES)
    counts = jnp.where(jnp.arange(DEVICES) == full_device, ROWS_DEV, counts).astype(jnp.int32)
    hottest = jax.random.randint(key_hot, (), 0, N_WIDE)
    offset = jax.random.randint(key_offset, (DEVICES, 1), 0, N_WIDE - 1)
    position = jnp.arange(ROWS_DEV, dtype=jnp.int32)[None, :]
    cyclic = (hottest + 1 + (offset + position) % (N_WIDE - 1)) % N_WIDE
    pattern = jnp.where(position < CAP, hottest, cyclic)
    noise = jax.random.randint(key_order, (DEVICES, ROWS_DEV), 0, 2 ** 16)
    score = jnp.where(position < counts[:, None], noise * ROWS_DEV + position, 2 ** 16 * ROWS_DEV + position)
    order = jnp.argsort(score, axis=1, stable=True)
    owner = jnp.take_along_axis(pattern, order, axis=1)
    return (counts, owner)


def passage_plan(key):
    counts, owner = route_plan(jax.random.fold_in(key, 7))
    within = jax.random.randint(jax.random.fold_in(key, 11), owner.shape, 0, LISTS_DEV)
    list_ids = (owner * LISTS_DEV + within).reshape(ROWS).astype(jnp.int32)
    codes = jax.random.randint(jax.random.fold_in(key, 13), (ROWS, M), 0, K).astype(jnp.int32)
    return (counts, list_ids, codes)


def clipped_normal(key, shape, scale, bound):
    return jnp.clip(scale * jax.random.normal(key, shape, jnp.float32), -bound, bound)


def centroid_field(key):
    sub = jax.random.fold_in(key, 17)
    return clipped_normal(sub, (LISTS, D), 1.0, 4.0)


def previous_words(key):
    sub = jax.random.fold_in(key, 19)
    return clipped_normal(sub, (M, K * DSUB), 1.0, 4.0)


def update_shift(key):
    sub = jax.random.fold_in(key, 23)
    return clipped_normal(sub, (M, K * DSUB), 0.5, 2.0)


def device_drift(key, index):
    sub = jax.random.fold_in(jax.random.fold_in(key, 31), index)
    ramp = index.astype(jnp.float32) / jnp.float32(DEVICES - 1)
    scale = 0.5 * jnp.exp(ramp * jnp.log(jnp.float32(6.0)))
    return scale * clipped_normal(sub, (D,), 1.0, 2.5)


def draw_rows(key, part):
    counts, list_ids, codes = passage_plan(key)
    centres = centroid_field(key).astype(jnp.bfloat16).astype(jnp.float32)
    moved = (previous_words(key) + update_shift(key)).reshape(M, K, DSUB)
    spaces = jnp.arange(M, dtype=jnp.int32)[None, :]
    noise_key = jax.random.fold_in(key, 29)

    def block(pieces):
        index, block_lists, block_codes = pieces
        sub = jax.random.fold_in(noise_key, index)
        noise = clipped_normal(sub, (ROWS_DEV, D), 0.3, 1.0)
        words = moved[spaces, block_codes].reshape(ROWS_DEV, D)
        drift = device_drift(key, index)[None, :]
        return (centres[block_lists] + words + noise + drift).astype(jnp.bfloat16)
    blocks = lax.map(block, (jnp.arange(DEVICES, dtype=jnp.int32), list_ids.reshape(DEVICES, ROWS_DEV), codes.reshape(DEVICES, ROWS_DEV, M)))
    return blocks.reshape(ROWS, D)


def draw_list_ids(key, part):
    counts, list_ids, codes = passage_plan(key)
    return list_ids


def draw_codes(key, part):
    counts, list_ids, codes = passage_plan(key)
    return codes


def draw_row_counts(key, part):
    counts, list_ids, codes = passage_plan(key)
    return counts.astype(jnp.int32)


def draw_centroids(key, part):
    return centroid_field(key).astype(jnp.bfloat16)


def draw_old_codebook(key, part):
    return previous_words(key)


def setup_inputs(seed: int = 0) -> dict:
    streams_of = jax.random.split(jax.random.key(seed), 7)
    rows = draw_rows(jax.random.fold_in(streams_of[6], 71), 0)
    list_ids = draw_list_ids(jax.random.fold_in(streams_of[6], 71), 0)
    codes = draw_codes(jax.random.fold_in(streams_of[6], 71), 0)
    row_counts = draw_row_counts(jax.random.fold_in(streams_of[6], 71), 0)
    centroids = draw_centroids(jax.random.fold_in(streams_of[6], 71), 0)
    old_codebook = draw_old_codebook(jax.random.fold_in(streams_of[6], 71), 0)
    return {"rows": rows, "list_ids": list_ids, "codes": codes, "row_counts": row_counts, "centroids": centroids, "old_codebook": old_codebook}


def reference(rows, list_ids, codes, row_counts, centroids, old_codebook):
    rows_b = rows.reshape(DEVICES, ROWS_DEV, D)
    lists_b = list_ids.reshape(DEVICES, ROWS_DEV)
    codes_b = codes.reshape(DEVICES, ROWS_DEV, M)
    position = jnp.arange(ROWS_DEV, dtype=jnp.int32)
    offsets = (jnp.arange(M, dtype=jnp.int32) * K)[None, :]

    def residual_of(block_rows, block_lists):
        return (block_rows.astype(jnp.float32) - centroids[block_lists].astype(jnp.float32)).astype(jnp.bfloat16)

    def absorb(carry, pieces):
        block_rows, block_lists, block_codes, count = pieces
        live_rows = (position < count).astype(jnp.float32)
        resid = residual_of(block_rows, block_lists).astype(jnp.float32) * live_rows[:, None]
        segment = (block_codes + offsets).reshape(ROWS_DEV * M)
        sums = carry[0] + jax.ops.segment_sum(resid.reshape(ROWS_DEV * M, DSUB), segment, num_segments=M * K)
        weights = jnp.broadcast_to(live_rows[:, None], (ROWS_DEV, M)).reshape(ROWS_DEV * M)
        counts = carry[1] + jax.ops.segment_sum(weights, segment, num_segments=M * K)
        return (sums, counts), None

    start = (jnp.zeros((M * K, DSUB), jnp.float32), jnp.zeros((M * K,), jnp.float32))
    (sums, counts), unused = lax.scan(absorb, start, (rows_b, lists_b, codes_b, row_counts))
    anchor = jnp.float32(ANCHOR)
    refit = (sums + anchor * old_codebook.reshape(M * K, DSUB)) / (counts[:, None] + anchor)
    table = refit.astype(jnp.bfloat16)

    def errors(pieces):
        block_rows, block_lists, block_codes, count = pieces
        resid = residual_of(block_rows, block_lists).astype(jnp.float32)
        segment = (block_codes + offsets).reshape(ROWS_DEV * M)
        decoded = table[segment].astype(jnp.float32).reshape(ROWS_DEV, D)
        diff = resid - decoded
        err = jnp.mean(diff * diff, axis=1)
        return jnp.where(position < count, err, jnp.float32(0.0))

    row_error = lax.map(errors, (rows_b, lists_b, codes_b, row_counts)).reshape(ROWS)
    return refit.reshape(M, K * DSUB), table.reshape(M, K * DSUB), row_error
```

```python
import functools

import jax
import jax.numpy as jnp
from jax import lax
from jax.experimental import pallas as pl
from jax.experimental.pallas import tpu as pltpu
from jax.sharding import PartitionSpec as P

K = 256
LO = 4
HI = K // LO
CHUNKS = 1
BLOCK = 512
VMEM = 56 * 1024 * 1024


def sums_kernel(lanes, rows_ref, cent_ref, hi_ref, low_ref, spread_ref, resid_ref, sums_ref, counts_ref, acc_ref, cacc_ref):
    step = pl.program_id(0)
    width = rows_ref.shape[1]
    spaces = hi_ref.shape[0]
    per = lanes // (width // spaces)
    block = rows_ref.shape[0]

    @pl.when(step == 0)
    def _():
        acc_ref[...] = jnp.zeros_like(acc_ref)
        cacc_ref[...] = jnp.zeros_like(cacc_ref)

    resid = (rows_ref[...].astype(jnp.float32) - cent_ref[...].astype(jnp.float32)).astype(jnp.bfloat16)
    resid_ref[...] = resid
    low = jnp.dot(low_ref[...], spread_ref[...], preferred_element_type=jnp.float32)
    level = lax.broadcasted_iota(jnp.int32, (HI, block), 0)
    zero = jnp.zeros((), jnp.bfloat16)
    for g in range(width // lanes):
        part = resid[:, g * lanes : (g + 1) * lanes]
        part_low = low[:, g * lanes : (g + 1) * lanes].astype(jnp.bfloat16)
        right = jnp.concatenate(
            [jnp.where(part_low == jnp.bfloat16(j), part, zero) for j in range(LO)], axis=1
        )
        left = jnp.concatenate(
            [
                (hi_ref[m : m + 1, :] == level).astype(jnp.float32).astype(jnp.bfloat16)
                for m in range(g * per, (g + 1) * per)
            ],
            axis=0,
        )
        acc_ref[g] += jnp.dot(left, right, preferred_element_type=jnp.float32)
        cacc_ref[g] += jnp.dot(left, low_ref[...], preferred_element_type=jnp.float32)

    @pl.when(step == pl.num_programs(0) - 1)
    def _():
        sub = lanes // per
        own = lax.broadcasted_iota(jnp.int32, (HI, lanes), 1) // sub
        for g in range(width // lanes):
            for j in range(LO):
                total = jnp.zeros((HI, lanes), jnp.float32)
                for m in range(per):
                    piece = acc_ref[g, m * HI : (m + 1) * HI, j * lanes : (j + 1) * lanes]
                    total = total + jnp.where(own == m, piece, 0.0)
                sums_ref[j * HI : (j + 1) * HI, g * lanes : (g + 1) * lanes] = total
        space = lax.broadcasted_iota(jnp.int32, (HI, LO * spaces), 1) % spaces
        total = jnp.zeros((HI, LO * spaces), jnp.float32)
        for g in range(width // lanes):
            for m in range(per):
                piece = cacc_ref[g, m * HI : (m + 1) * HI, :]
                total = total + jnp.where(space == g * per + m, piece, 0.0)
        counts_ref[...] = total


def error_kernel(lanes, resid_ref, hi_ref, low_ref, spread_ref, widen_ref, table_ref, err_ref, diag_ref):
    step = pl.program_id(0)
    width = resid_ref.shape[1]
    spaces = hi_ref.shape[1]
    sub = width // spaces
    per = lanes // sub
    block = resid_ref.shape[0]

    @pl.when(step == 0)
    def _():
        own = lax.broadcasted_iota(jnp.int32, (HI, lanes), 1) // sub
        for g in range(width // lanes):
            for j in range(LO):
                piece = table_ref[j * HI : (j + 1) * HI, g * lanes : (g + 1) * lanes].astype(jnp.float32)
                for m in range(per):
                    diag_ref[g, m * HI : (m + 1) * HI, j * lanes : (j + 1) * lanes] = jnp.where(
                        own == m, piece, 0.0
                    ).astype(jnp.bfloat16)

    low = jnp.dot(low_ref[...], spread_ref[...], preferred_element_type=jnp.float32)
    level = (lax.broadcasted_iota(jnp.int32, (block, per * HI), 1) % HI).astype(jnp.float32)
    total = jnp.zeros((block, lanes), jnp.float32)
    for g in range(width // lanes):
        high = jnp.dot(
            hi_ref[...], widen_ref[:, g * per * HI : (g + 1) * per * HI], preferred_element_type=jnp.float32
        )
        pick = (high == level).astype(jnp.float32).astype(jnp.bfloat16)
        words = jnp.dot(pick, diag_ref[g], preferred_element_type=jnp.float32)
        part_low = low[:, g * lanes : (g + 1) * lanes]
        decoded = words[:, :lanes]
        for j in range(1, LO):
            decoded = jnp.where(part_low == float(j), words[:, j * lanes : (j + 1) * lanes], decoded)
        diff = resid_ref[:, g * lanes : (g + 1) * lanes].astype(jnp.float32) - decoded
        total = total + diff * diff
    err_ref[0] = jnp.sum(total.T, axis=0, keepdims=True)


def codeword_sums(rows, cent, hi_cols, low_hot, spread):
    total, width = rows.shape
    spaces = hi_cols.shape[0]
    lanes = min(128, width)
    per = lanes // (width // spaces)
    groups = width // lanes
    row_block = pl.BlockSpec((BLOCK, width), lambda i: (i, 0))
    return pl.pallas_call(
        functools.partial(sums_kernel, lanes),
        grid=(total // BLOCK,),
        in_specs=[
            row_block,
            row_block,
            pl.BlockSpec((spaces, BLOCK), lambda i: (0, i)),
            pl.BlockSpec((BLOCK, LO * spaces), lambda i: (i, 0)),
            pl.BlockSpec((LO * spaces, width), lambda i: (0, 0)),
        ],
        out_specs=[
            row_block,
            pl.BlockSpec((K, width), lambda i: (0, 0)),
            pl.BlockSpec((HI, LO * spaces), lambda i: (0, 0)),
        ],
        out_shape=[
            jax.ShapeDtypeStruct((total, width), jnp.bfloat16),
            jax.ShapeDtypeStruct((K, width), jnp.float32),
            jax.ShapeDtypeStruct((HI, LO * spaces), jnp.float32),
        ],
        scratch_shapes=[
            pltpu.VMEM((groups, per * HI, LO * lanes), jnp.float32),
            pltpu.VMEM((groups, per * HI, LO * spaces), jnp.float32),
        ],
        compiler_params=pltpu.CompilerParams(vmem_limit_bytes=VMEM),
        cost_estimate=pl.CostEstimate(
            flops=2 * total * per * HI * LO * width, bytes_accessed=6 * total * width, transcendentals=0
        ),
        name="codeword_sums",
    )(rows, cent, hi_cols, low_hot, spread)


def squared_errors(resid, hi_rows, low_hot, spread, widen, table):
    total, width = resid.shape
    spaces = hi_rows.shape[1]
    lanes = min(128, width)
    per = lanes // (width // spaces)
    groups = width // lanes
    whole = lambda a: pl.BlockSpec(a.shape, lambda i: (0, 0))
    return pl.pallas_call(
        functools.partial(error_kernel, lanes),
        grid=(total // BLOCK,),
        in_specs=[
            pl.BlockSpec((BLOCK, width), lambda i: (i, 0)),
            pl.BlockSpec((BLOCK, spaces), lambda i: (i, 0)),
            pl.BlockSpec((BLOCK, LO * spaces), lambda i: (i, 0)),
            whole(spread),
            whole(widen),
            whole(table),
        ],
        out_specs=pl.BlockSpec((1, 1, BLOCK), lambda i: (i, 0, 0)),
        out_shape=jax.ShapeDtypeStruct((total // BLOCK, 1, BLOCK), jnp.float32),
        scratch_shapes=[pltpu.VMEM((groups, per * HI, LO * lanes), jnp.bfloat16)],
        compiler_params=pltpu.CompilerParams(vmem_limit_bytes=VMEM),
        cost_estimate=pl.CostEstimate(
            flops=2 * total * per * HI * LO * width, bytes_accessed=2 * total * width, transcendentals=0
        ),
        name="squared_errors",
    )(resid, hi_rows, low_hot, spread, widen, table).reshape(total)


def body(rows, list_ids, codes, row_counts, centroids, old_codebook):
    local_rows, width_d = rows.shape
    spaces = codes.shape[1]
    sub = width_d // spaces
    wide_count = lax.axis_size("wide")
    narrow_count = lax.axis_size("narrow")
    core = lax.axis_index("narrow")
    own_wide = lax.axis_index("wide")
    anchor = float(local_rows * narrow_count * wide_count // (4 * K))
    half = width_d // narrow_count
    half_spaces = spaces // narrow_count
    swap = [(0, 1), (1, 0)]

    mine = lambda a, n: lax.dynamic_slice_in_dim(a, core * n, n, 1)
    others = lambda a, n: lax.dynamic_slice_in_dim(a, (1 - core) * n, n, 1)
    width = half // CHUNKS
    chunk_spaces = half_spaces // CHUNKS
    own_cent = mine(centroids, half)
    gathered = [
        lax.all_gather(own_cent[:, c * width : (c + 1) * width], "wide", axis=0, tiled=True) for c in range(CHUNKS)
    ]

    is_live = jnp.arange(local_rows, dtype=jnp.int32) < row_counts[0]
    keyed = jnp.where(is_live[:, None], codes, 4 * K)
    both_rows = jnp.concatenate([mine(rows, half), lax.ppermute(others(rows, half), "narrow", swap)])
    both_codes = jnp.concatenate(
        [mine(keyed, half_spaces), lax.ppermute(others(keyed, half_spaces), "narrow", swap)]
    )
    both_lists = jnp.concatenate([list_ids, lax.ppermute(list_ids, "narrow", swap)])
    total = both_rows.shape[0]
    hi = both_codes // LO
    low = both_codes % LO
    old = mine(old_codebook.reshape(1, spaces, HI, LO, sub), half_spaces)
    old = old.reshape(half_spaces, HI, LO, sub).transpose(2, 1, 0, 3).reshape(K, half)

    feature = jnp.arange(width, dtype=jnp.int32) // sub
    space = jnp.arange(chunk_spaces, dtype=jnp.int32)
    expand = (feature[None, :] == space[:, None]).astype(jnp.float32)
    level = jnp.arange(LO, dtype=jnp.float32)
    spread = (level[:, None, None] * expand[None]).reshape(LO * chunk_spaces, width).astype(jnp.bfloat16)
    widen = jnp.repeat(jnp.eye(chunk_spaces, dtype=jnp.bfloat16), HI, axis=1)

    errs = jnp.zeros((total,), jnp.float32)
    books = []
    for c in range(CHUNKS):
        cols = slice(c * width, (c + 1) * width)
        spc = slice(c * chunk_spaces, (c + 1) * chunk_spaces)
        low_hot = (low[:, None, spc] == jnp.arange(LO, dtype=jnp.int32)[None, :, None]).astype(jnp.bfloat16)
        low_hot = low_hot.reshape(total, LO * chunk_spaces)
        cent = gathered[c].at[both_lists].get(mode="clip")
        resid, sums, counts = codeword_sums(both_rows[:, cols], cent, hi[:, spc].T, low_hot, spread)
        sums, counts = lax.psum((sums, counts), "wide")
        counts = counts.reshape(HI, LO, chunk_spaces).transpose(1, 0, 2).reshape(K, chunk_spaces)
        weight = jnp.dot(counts + anchor, expand, precision=lax.Precision.HIGHEST)
        book = (sums + anchor * old[:, cols]) / weight
        errs = errs + squared_errors(
            resid, hi[:, spc].astype(jnp.bfloat16), low_hot, spread, widen, book.astype(jnp.bfloat16)
        )
        books.append(book)
    book = jnp.concatenate(books, axis=1) if CHUNKS > 1 else books[0]
    book = book.reshape(LO, HI, half_spaces, sub).transpose(2, 1, 0, 3).reshape(half_spaces, K * sub)
    codebook = lax.all_gather(book, "narrow", axis=0, tiled=True)
    share = spaces // wide_count
    search_table = lax.dynamic_slice_in_dim(codebook, own_wide * share, share, 0).astype(jnp.bfloat16)
    err = errs[:local_rows] + lax.ppermute(errs[local_rows:], "narrow", swap)
    err = jnp.where(is_live, err / width_d, 0.0)
    return (codebook, search_table, err)


def solution(mesh):
    in_specs = (
        P(("narrow", "wide"), None),
        P(("narrow", "wide")),
        P(("narrow", "wide"), None),
        P(("narrow", "wide")),
        P("wide", None),
        P(),
    )
    out_specs = (P(), P("wide", None), P(("narrow", "wide")))
    return jax.shard_map(body, mesh=mesh, in_specs=in_specs, out_specs=out_specs, check_vma=False)
```

```python
import functools

import jax
import jax.numpy as jnp
from jax import lax
from jax.experimental import pallas as pl
from jax.experimental.pallas import tpu as pltpu
from jax.sharding import PartitionSpec as P

K = 256
LO = 4
HI = K // LO
CHUNKS = 1
BLOCK = 512
VMEM = 56 * 1024 * 1024


def sums_kernel(lanes, rows_ref, cent_ref, hi_ref, low_ref, spread_ref, resid_ref, sums_ref, counts_ref, acc_ref, cacc_ref):
    step = pl.program_id(0)
    width = rows_ref.shape[1]
    spaces = hi_ref.shape[0]
    per = lanes // (width // spaces)
    block = rows_ref.shape[0]

    @pl.when(step == 0)
    def _():
        acc_ref[...] = jnp.zeros_like(acc_ref)
        cacc_ref[...] = jnp.zeros_like(cacc_ref)

    resid = (rows_ref[...].astype(jnp.float32) - cent_ref[...].astype(jnp.float32)).astype(jnp.bfloat16)
    resid_ref[...] = resid
    low = jnp.dot(low_ref[...], spread_ref[...], preferred_element_type=jnp.float32)
    level = lax.broadcasted_iota(jnp.int32, (HI, block), 0)
    zero = jnp.zeros((), jnp.bfloat16)
    for g in range(width // lanes):
        part = resid[:, g * lanes : (g + 1) * lanes]
        part_low = low[:, g * lanes : (g + 1) * lanes].astype(jnp.bfloat16)
        right = jnp.concatenate(
            [jnp.where(part_low == jnp.bfloat16(j), part, zero) for j in range(LO)], axis=1
        )
        left = jnp.concatenate(
            [
                (hi_ref[m : m + 1, :] == level).astype(jnp.float32).astype(jnp.bfloat16)
                for m in range(g * per, (g + 1) * per)
            ],
            axis=0,
        )
        acc_ref[g] += jnp.dot(left, right, preferred_element_type=jnp.float32)
        cacc_ref[g] += jnp.dot(left, low_ref[...], preferred_element_type=jnp.float32)

    @pl.when(step == pl.num_programs(0) - 1)
    def _():
        sub = lanes // per
        own = lax.broadcasted_iota(jnp.int32, (HI, lanes), 1) // sub
        for g in range(width // lanes):
            for j in range(LO):
                total = jnp.zeros((HI, lanes), jnp.float32)
                for m in range(per):
                    piece = acc_ref[g, m * HI : (m + 1) * HI, j * lanes : (j + 1) * lanes]
                    total = total + jnp.where(own == m, piece, 0.0)
                sums_ref[j * HI : (j + 1) * HI, g * lanes : (g + 1) * lanes] = total
        space = lax.broadcasted_iota(jnp.int32, (HI, LO * spaces), 1) % spaces
        total = jnp.zeros((HI, LO * spaces), jnp.float32)
        for g in range(width // lanes):
            for m in range(per):
                piece = cacc_ref[g, m * HI : (m + 1) * HI, :]
                total = total + jnp.where(space == g * per + m, piece, 0.0)
        counts_ref[...] = total


def error_kernel(lanes, resid_ref, hi_ref, low_ref, spread_ref, widen_ref, table_ref, err_ref, diag_ref):
    step = pl.program_id(0)
    width = resid_ref.shape[1]
    spaces = hi_ref.shape[1]
    sub = width // spaces
    per = lanes // sub
    block = resid_ref.shape[0]

    @pl.when(step == 0)
    def _():
        own = lax.broadcasted_iota(jnp.int32, (HI, lanes), 1) // sub
        for g in range(width // lanes):
            for j in range(LO):
                piece = table_ref[j * HI : (j + 1) * HI, g * lanes : (g + 1) * lanes].astype(jnp.float32)
                for m in range(per):
                    diag_ref[g, m * HI : (m + 1) * HI, j * lanes : (j + 1) * lanes] = jnp.where(
                        own == m, piece, 0.0
                    ).astype(jnp.bfloat16)

    low = jnp.dot(low_ref[...], spread_ref[...], preferred_element_type=jnp.float32)
    level = (lax.broadcasted_iota(jnp.int32, (block, per * HI), 1) % HI).astype(jnp.float32)
    total = jnp.zeros((block, lanes), jnp.float32)
    for g in range(width // lanes):
        high = jnp.dot(
            hi_ref[...], widen_ref[:, g * per * HI : (g + 1) * per * HI], preferred_element_type=jnp.float32
        )
        pick = (high == level).astype(jnp.float32).astype(jnp.bfloat16)
        words = jnp.dot(pick, diag_ref[g], preferred_element_type=jnp.float32)
        part_low = low[:, g * lanes : (g + 1) * lanes]
        decoded = words[:, :lanes]
        for j in range(1, LO):
            decoded = jnp.where(part_low == float(j), words[:, j * lanes : (j + 1) * lanes], decoded)
        diff = resid_ref[:, g * lanes : (g + 1) * lanes].astype(jnp.float32) - decoded
        total = total + diff * diff
    err_ref[0] = jnp.sum(total.T, axis=0, keepdims=True)


def reduce_kernel(n, x_ref, out_ref, got, full, send1, recv1, send2, recv2):
    me = lax.axis_index("wide")
    core = lax.axis_index("narrow")
    barrier = pltpu.get_barrier_semaphore()

    def greet(k, _):
        pl.semaphore_signal(
            barrier, inc=1, device_id=(core, lax.rem(me + k, n)), device_id_type=pl.DeviceIdType.MESH
        )
        return 0

    lax.fori_loop(1, n, greet, 0)
    pl.semaphore_wait(barrier, n - 1)

    def part(k):
        peer = lax.rem(me + k, n)
        return pltpu.make_async_remote_copy(
            src_ref=x_ref.at[peer],
            dst_ref=got.at[k],
            send_sem=send1.at[k],
            recv_sem=recv1.at[k],
            device_id=(core, peer),
            device_id_type=pl.DeviceIdType.MESH,
        )

    def share(k, slot):
        return pltpu.make_async_remote_copy(
            src_ref=full.at[slot],
            dst_ref=full.at[slot],
            send_sem=send2.at[k],
            recv_sem=recv2.at[k],
            device_id=(core, lax.rem(me + k, n)),
            device_id_type=pl.DeviceIdType.MESH,
        )

    def each(act):
        def step(k, _):
            act(k)
            return 0

        lax.fori_loop(1, n, step, 0)

    each(lambda k: part(k).start())

    def add(k, total):
        part(k).wait_recv()
        return total + got[k]

    full[me] = lax.fori_loop(1, n, add, x_ref[me])
    each(lambda k: share(k, me).start())
    each(lambda k: share(k, lax.rem(me - k + n, n)).wait_recv())
    each(lambda k: part(k).wait_send())
    each(lambda k: share(k, me).wait_send())
    out_ref[...] = full[...]


def reduce_wide(sums, counts, n):
    width = sums.shape[1]
    rows_s, rows_c = sums.shape[0] // n, counts.shape[0] // n
    pad = -(rows_s + rows_c) % 8
    counts_in = jnp.pad(
        counts.reshape(n, rows_c, counts.shape[1]), ((0, 0), (0, pad), (0, width - counts.shape[1]))
    )
    parts = jnp.concatenate([sums.reshape(n, rows_s, width), counts_in], axis=1)
    full = pl.pallas_call(
        functools.partial(reduce_kernel, n),
        out_shape=jax.ShapeDtypeStruct(parts.shape, parts.dtype),
        in_specs=[pl.BlockSpec(memory_space=pltpu.VMEM)],
        out_specs=pl.BlockSpec(memory_space=pltpu.VMEM),
        scratch_shapes=[
            pltpu.VMEM(parts.shape, parts.dtype),
            pltpu.VMEM(parts.shape, parts.dtype),
        ]
        + [pltpu.SemaphoreType.DMA((n,))] * 4,
        compiler_params=pltpu.CompilerParams(
            collective_id=0, has_side_effects=True, vmem_limit_bytes=24 * 1024 * 1024
        ),
        name="reduce_wide",
    )(parts)
    return (
        full[:, :rows_s].reshape(sums.shape),
        full[:, rows_s : rows_s + rows_c, : counts.shape[1]].reshape(counts.shape),
    )


def codeword_sums(rows, cent, hi_cols, low_hot, spread):
    total, width = rows.shape
    spaces = hi_cols.shape[0]
    lanes = min(128, width)
    per = lanes // (width // spaces)
    groups = width // lanes
    row_block = pl.BlockSpec((BLOCK, width), lambda i: (i, 0))
    return pl.pallas_call(
        functools.partial(sums_kernel, lanes),
        grid=(total // BLOCK,),
        in_specs=[
            row_block,
            row_block,
            pl.BlockSpec((spaces, BLOCK), lambda i: (0, i)),
            pl.BlockSpec((BLOCK, LO * spaces), lambda i: (i, 0)),
            pl.BlockSpec((LO * spaces, width), lambda i: (0, 0)),
        ],
        out_specs=[
            row_block,
            pl.BlockSpec((K, width), lambda i: (0, 0)),
            pl.BlockSpec((HI, LO * spaces), lambda i: (0, 0)),
        ],
        out_shape=[
            jax.ShapeDtypeStruct((total, width), jnp.bfloat16),
            jax.ShapeDtypeStruct((K, width), jnp.float32),
            jax.ShapeDtypeStruct((HI, LO * spaces), jnp.float32),
        ],
        scratch_shapes=[
            pltpu.VMEM((groups, per * HI, LO * lanes), jnp.float32),
            pltpu.VMEM((groups, per * HI, LO * spaces), jnp.float32),
        ],
        compiler_params=pltpu.CompilerParams(vmem_limit_bytes=VMEM),
        cost_estimate=pl.CostEstimate(
            flops=2 * total * per * HI * LO * width, bytes_accessed=6 * total * width, transcendentals=0
        ),
        name="codeword_sums",
    )(rows, cent, hi_cols, low_hot, spread)


def squared_errors(resid, hi_rows, low_hot, spread, widen, table):
    total, width = resid.shape
    spaces = hi_rows.shape[1]
    lanes = min(128, width)
    per = lanes // (width // spaces)
    groups = width // lanes
    whole = lambda a: pl.BlockSpec(a.shape, lambda i: (0, 0))
    return pl.pallas_call(
        functools.partial(error_kernel, lanes),
        grid=(total // BLOCK,),
        in_specs=[
            pl.BlockSpec((BLOCK, width), lambda i: (i, 0)),
            pl.BlockSpec((BLOCK, spaces), lambda i: (i, 0)),
            pl.BlockSpec((BLOCK, LO * spaces), lambda i: (i, 0)),
            whole(spread),
            whole(widen),
            whole(table),
        ],
        out_specs=pl.BlockSpec((1, 1, BLOCK), lambda i: (i, 0, 0)),
        out_shape=jax.ShapeDtypeStruct((total // BLOCK, 1, BLOCK), jnp.float32),
        scratch_shapes=[pltpu.VMEM((groups, per * HI, LO * lanes), jnp.bfloat16)],
        compiler_params=pltpu.CompilerParams(vmem_limit_bytes=VMEM),
        cost_estimate=pl.CostEstimate(
            flops=2 * total * per * HI * LO * width, bytes_accessed=2 * total * width, transcendentals=0
        ),
        name="squared_errors",
    )(resid, hi_rows, low_hot, spread, widen, table).reshape(total)


def body(rows, list_ids, codes, row_counts, centroids, old_codebook):
    local_rows, width_d = rows.shape
    spaces = codes.shape[1]
    sub = width_d // spaces
    wide_count = lax.axis_size("wide")
    narrow_count = lax.axis_size("narrow")
    core = lax.axis_index("narrow")
    own_wide = lax.axis_index("wide")
    anchor = float(local_rows * narrow_count * wide_count // (4 * K))
    half = width_d // narrow_count
    half_spaces = spaces // narrow_count
    swap = [(0, 1), (1, 0)]

    mine = lambda a, n: lax.dynamic_slice_in_dim(a, core * n, n, 1)
    others = lambda a, n: lax.dynamic_slice_in_dim(a, (1 - core) * n, n, 1)
    width = half // CHUNKS
    chunk_spaces = half_spaces // CHUNKS
    own_cent = mine(centroids, half)
    gathered = [
        lax.all_gather(own_cent[:, c * width : (c + 1) * width], "wide", axis=0, tiled=True) for c in range(CHUNKS)
    ]

    is_live = jnp.arange(local_rows, dtype=jnp.int32) < row_counts[0]
    keyed = jnp.where(is_live[:, None], codes, 4 * K)
    both_rows = jnp.concatenate([mine(rows, half), lax.ppermute(others(rows, half), "narrow", swap)])
    both_codes = jnp.concatenate(
        [mine(keyed, half_spaces), lax.ppermute(others(keyed, half_spaces), "narrow", swap)]
    )
    both_lists = jnp.concatenate([list_ids, lax.ppermute(list_ids, "narrow", swap)])
    total = both_rows.shape[0]
    hi = both_codes // LO
    low = both_codes % LO
    old = mine(old_codebook.reshape(1, spaces, HI, LO, sub), half_spaces)
    old = old.reshape(half_spaces, HI, LO, sub).transpose(2, 1, 0, 3).reshape(K, half)

    feature = jnp.arange(width, dtype=jnp.int32) // sub
    space = jnp.arange(chunk_spaces, dtype=jnp.int32)
    expand = (feature[None, :] == space[:, None]).astype(jnp.float32)
    level = jnp.arange(LO, dtype=jnp.float32)
    spread = (level[:, None, None] * expand[None]).reshape(LO * chunk_spaces, width).astype(jnp.bfloat16)
    widen = jnp.repeat(jnp.eye(chunk_spaces, dtype=jnp.bfloat16), HI, axis=1)

    errs = jnp.zeros((total,), jnp.float32)
    books = []
    for c in range(CHUNKS):
        cols = slice(c * width, (c + 1) * width)
        spc = slice(c * chunk_spaces, (c + 1) * chunk_spaces)
        low_hot = (low[:, None, spc] == jnp.arange(LO, dtype=jnp.int32)[None, :, None]).astype(jnp.bfloat16)
        low_hot = low_hot.reshape(total, LO * chunk_spaces)
        cent = gathered[c].at[both_lists].get(mode="clip")
        resid, sums, counts = codeword_sums(both_rows[:, cols], cent, hi[:, spc].T, low_hot, spread)
        sums, counts = reduce_wide(sums, counts, wide_count)
        counts = counts.reshape(HI, LO, chunk_spaces).transpose(1, 0, 2).reshape(K, chunk_spaces)
        weight = jnp.dot(counts + anchor, expand, precision=lax.Precision.HIGHEST)
        book = (sums + anchor * old[:, cols]) / weight
        errs = errs + squared_errors(
            resid, hi[:, spc].astype(jnp.bfloat16), low_hot, spread, widen, book.astype(jnp.bfloat16)
        )
        books.append(book)
    book = jnp.concatenate(books, axis=1) if CHUNKS > 1 else books[0]
    book = book.reshape(LO, HI, half_spaces, sub).transpose(2, 1, 0, 3).reshape(half_spaces, K * sub)
    codebook = lax.all_gather(book, "narrow", axis=0, tiled=True)
    share = spaces // wide_count
    search_table = lax.dynamic_slice_in_dim(codebook, own_wide * share, share, 0).astype(jnp.bfloat16)
    err = errs[:local_rows] + lax.ppermute(errs[local_rows:], "narrow", swap)
    err = jnp.where(is_live, err / width_d, 0.0)
    return (codebook, search_table, err)


def solution(mesh):
    in_specs = (
        P(("narrow", "wide"), None),
        P(("narrow", "wide")),
        P(("narrow", "wide"), None),
        P(("narrow", "wide")),
        P("wide", None),
        P(),
    )
    out_specs = (P(), P("wide", None), P(("narrow", "wide")))
    return jax.shard_map(body, mesh=mesh, in_specs=in_specs, out_specs=out_specs, check_vma=False)
```
